32 devices in a mesh: dp: 4 (over y, x), expert: 8 (over z, core).
Axes of the slice: x: 2, y: 2, z: 4, core: 2. Of those that a mesh axis runs over, the one named last changes fastest.
Arguments:
- features: bfloat16 [8192, 512], P(('dp', 'expert')), may hold values from -6 to 6
- slots: int32 [8192], P(('dp', 'expert')), may hold values from 0 to 31
- routes: int32 [8192, 2], P(('dp', 'expert')), may hold values from 0 to 7, all different within a row; in each aligned block of 256 rows (0 to 255, 256 to 511, ...) at most 128 rows name the same one
- cotangent: bfloat16 [8192, 512], P(('dp', 'expert')), may hold values from -1.5 to 1.5
- pos_table: bfloat16 [32, 64], replicated, may hold values from -6 to 6
- tower_in: bfloat16 [64, 256], replicated, may hold values from -0.75 to 0.75
- tower_out: bfloat16 [256, 512], replicated, may hold values from -0.375 to 0.375
- router: bfloat16 [512, 8], replicated, may hold values from -0.5 to 0.5
- w_up: bfloat16 [8, 512, 2048], P('expert'), may hold values from -0.25 to 0.25
- w_down: bfloat16 [8, 2048, 512], P('expert'), may hold values from -0.125 to 0.125
Outputs:
- layer_out: bfloat16 [8192, 512], P(('dp', 'expert'))
- grad_in: bfloat16 [8192, 512], P(('dp', 'expert'))
- grad_up: bfloat16 [8, 512, 2048], P('expert')
- grad_down: bfloat16 [8, 2048, 512], P('expert')
The draws below stay inside these ranges and needn't reach their ends.
Inputs may be any that keep to these rules, and one draw needn't show every extreme that they name: `routes`: within the rows of one device no expert is named by more than 128 rows; in some devices' rows one expert is named by exactly 128.
All inputs are finite; a program needn't handle non-finite values.
Results may differ from the reference program's by a relative error of at most 0.013.
Values may be sent and summed in bfloat16 or wider, within the bound.
A program may use at most 128 MiB of HBM per device.

```python
import math
import jax
import jax.numpy as jnp
import numpy as np
from jax import lax

D = 512
H = 2048
PE = 64
TW = 256
SLOTS = 32
TOP = 2
TOK_DEV = 256
EXPERTS = 8
CAP = 128
TOKENS = 8192
N_DP = 4
N_EXPERT = 8


def place_ends(values, key, least, high):
    dims = values.shape
    index_at = [jax.random.randint(jax.random.fold_in(key, axis), (), 0, dims[axis]) for axis in range(len(dims))]
    values = values.at[tuple(index_at)].set(least)
    longest = dims.index(max(dims))
    index_at[longest] = (index_at[longest] + 1) % dims[longest]
    return values.at[tuple(index_at)].set(high)


def block_scale(own_key, shape, pieces, least, high):
    gain, own = 1.0, jax.random.fold_in(own_key, 6)
    for dim, blocks in pieces:
        heights = jnp.exp(jax.random.uniform(jax.random.fold_in(own, dim), (blocks,), jnp.float32, least / len(pieces), high / len(pieces)))
        gain = gain * jnp.repeat(heights, shape[dim] // blocks).reshape([-1 if axis == dim else 1 for axis in range(len(shape))])
    return gain


def deal_out(rng, own, number, rows, amount, top, limit, slope):
    order = jax.random.permutation(rng, amount)
    crowded, usual = portions_of(amount, rows * top, limit, slope, True), portions_of(amount, rows * top, limit, slope, False)
    places = jnp.arange(amount)

    def named(sizes, turn):
        used = int((sizes > 0).sum())
        fixed = max(1, used // 4)
        passed = fixed + (places - fixed + turn * (used - fixed)) % max(1, amount - fixed)
        return jnp.zeros((amount,), jnp.int32).at[order[jnp.where(places < fixed, places, passed)]].set(jnp.asarray(sizes, jnp.int32))

    sizes = jnp.where(number % 4 == 0, named(crowded, number // 4), named(usual, number - number // 4 - 1))
    mixed = jax.random.permutation(jax.random.fold_in(own, 3), amount)
    giver, sink = mixed[0:amount // 2 * 2:2], mixed[1:amount // 2 * 2:2]
    slack = jnp.minimum(sizes[giver] - 1, limit - sizes[sink]) // 2
    slack = jnp.where((giver == order[0]) | (sink == order[0]) | (sizes[sink] == 0), 0, jnp.maximum(slack, 0))
    passed = jax.random.randint(jax.random.fold_in(own, 4), (amount // 2,), 0, 1 << 20) % (slack + 1)
    sizes = sizes.at[giver].add(-passed).at[sink].add(passed)
    members = jnp.searchsorted(jnp.cumsum(sizes), jnp.arange(rows * top), side="right").astype(jnp.int32)
    table = members.reshape(top, rows).T
    table = table[jax.random.permutation(jax.random.fold_in(own, 1), rows)]
    turn = jax.random.randint(jax.random.fold_in(own, 2), (rows, 1), 0, top)
    return jnp.take_along_axis(table, (jnp.arange(top)[None, :] + turn) % top, axis=1)


def portions_of(amount, total, reach, slope, full):
    weights = [(1 << 20) // math.isqrt(standing ** slope) + 1 for standing in range(1, amount + 1)]
    largest = reach if full else min(reach, max(-(-total // amount), total * weights[0] // sum(weights)))
    least = 1 if total - largest >= amount - 1 else 0
    counts, surplus = [largest] + [least] * (amount - 1), total - largest - least * (amount - 1)
    while surplus > 0:
        free = [i for i in range(1, amount) if counts[i] < largest] or [i for i in range(1, amount) if counts[i] < reach]
        mass, remaining = sum([weights[i] for i in free]), surplus
        for i in free:
            extra = min(reach - counts[i], max(1, remaining * weights[i] // mass), surplus)
            counts[i] = counts[i] + extra
            surplus = surplus - extra
    return np.array(counts)


def normal_values(stream_key, shape, deviation, reach, cuts=(), kind=jnp.bfloat16):
    entries = deviation * jax.random.normal(stream_key, shape, jnp.float32)
    if cuts:
        entries = entries * block_scale(stream_key, shape, cuts, -0.22, 0.18)
    return jnp.clip(entries, -reach, reach).astype(kind)


def setup_inputs(seed: int = 0) -> dict:
    splits = jax.random.split(jax.random.key(seed), 11)
    features = normal_values(splits[0], (TOKENS, D), 1.0, 6.0, ((0, 32),))
    slots = place_ends(jax.random.randint(splits[1], (TOKENS,), 0, SLOTS), jax.random.fold_in(splits[1], 1), 0, SLOTS - 1).astype(jnp.int32)
    routes_keys = jax.random.split(jax.random.fold_in(splits[2], 1), TOKENS // TOK_DEV)
    routes_turns = jax.random.permutation(jax.random.fold_in(splits[2], 3), TOKENS // TOK_DEV)
    routes = jax.vmap(lambda own, number: deal_out(jax.random.fold_in(splits[2], 2), own, number, TOK_DEV, EXPERTS, TOP, CAP, 2))(routes_keys, routes_turns).reshape((TOKENS, TOP))
    cotangent = normal_values(splits[3], (TOKENS, D), 0.25, 1.5, ((0, 32),))
    pos_table = normal_values(splits[4], (SLOTS, PE), 1.0, 6.0)
    tower_in = normal_values(splits[5], (PE, TW), PE ** -0.5, 0.75)
    tower_out = normal_values(splits[6], (TW, D), TW ** -0.5, 0.375)
    router = normal_values(splits[7], (D, EXPERTS), (D // 4) ** -0.5, 0.5)
    w_up = normal_values(splits[8], (EXPERTS, D, H), D ** -0.5, 0.25, ((0, 8),))
    w_down = normal_values(splits[9], (EXPERTS, H, D), H ** -0.5, 0.125, ((0, 8),))
    return {"features": features, "slots": slots, "routes": routes, "cotangent": cotangent, "pos_table": pos_table, "tower_in": tower_in, "tower_out": tower_out, "router": router, "w_up": w_up, "w_down": w_down}


coef_a = 0.7978845608028654
coef_b = 0.044715


def gelu_pair(pre_act):
    inner = coef_a * (pre_act + coef_b * pre_act * pre_act * pre_act)
    tanh_val = jnp.tanh(inner)
    activated = 0.5 * pre_act * (1.0 + tanh_val)
    gelu_slope = 0.5 * (1.0 + tanh_val) + 0.5 * pre_act * (1.0 - tanh_val * tanh_val) * coef_a * (1.0 + 3.0 * coef_b * pre_act * pre_act)
    return activated, gelu_slope


def expert_pass(packed):
    inputs_rows, cot_rows, w_up_one, w_down_one = packed
    pre_act = jnp.dot(inputs_rows, w_up_one, preferred_element_type=jnp.float32)
    activated, gelu_slope = gelu_pair(pre_act)
    hidden = activated.astype(jnp.bfloat16)
    outputs = jnp.dot(hidden, w_down_one, preferred_element_type=jnp.float32).astype(jnp.bfloat16)
    d_hidden = jnp.dot(cot_rows, w_down_one.T, preferred_element_type=jnp.float32)
    d_pre = (d_hidden * gelu_slope).astype(jnp.bfloat16)
    grad_down_part = jnp.dot(hidden.T, cot_rows, preferred_element_type=jnp.float32).astype(jnp.bfloat16)
    grad_up_part = jnp.dot(inputs_rows.T, d_pre, preferred_element_type=jnp.float32).astype(jnp.bfloat16)
    d_inputs = jnp.dot(d_pre, w_up_one.T, preferred_element_type=jnp.float32).astype(jnp.bfloat16)
    return outputs, d_inputs, grad_up_part, grad_down_part


def reference(features, slots, routes, cotangent, pos_table, tower_in, tower_out, router, w_up, w_down):
    pos_hidden = jax.nn.relu(jnp.dot(pos_table, tower_in, preferred_element_type=jnp.float32))
    pos_rows = jnp.dot(pos_hidden, tower_out.astype(jnp.float32), precision=lax.Precision.HIGHEST)
    mixed_in = (features.astype(jnp.float32) + pos_rows[slots]).astype(jnp.bfloat16)
    logits = jnp.dot(mixed_in, router, preferred_element_type=jnp.float32)
    chosen = jnp.take_along_axis(logits, routes, axis=1)
    squashed = 1.0 / (1.0 + jnp.exp(-chosen))
    gate_total = jnp.sum(squashed, axis=1, keepdims=True)
    gates = squashed / gate_total
    cot_wide = cotangent.astype(jnp.float32)
    slot_cot = (gates[:, :, None] * cot_wide[:, None, :]).astype(jnp.bfloat16)
    group_rows = N_EXPERT * TOK_DEV
    span = N_EXPERT * CAP
    expert_ids = jnp.arange(EXPERTS, dtype=jnp.int32)
    out_blocks = []
    grad_blocks = []
    up_total = jnp.zeros((EXPERTS, D, H), jnp.float32)
    down_total = jnp.zeros((EXPERTS, H, D), jnp.float32)
    for group_index in range(N_DP):
        first_row = group_index * group_rows
        block_routes = routes[first_row:first_row + group_rows].reshape(-1)
        block_hot = (block_routes[:, None] == expert_ids[None, :]).astype(jnp.int32)
        before = jnp.cumsum(block_hot, axis=0, dtype=jnp.int32) - block_hot
        slot_rank = jnp.sum(before * block_hot, axis=1, dtype=jnp.int32).astype(jnp.int32)
        slot_place = (block_routes * span + slot_rank).astype(jnp.int32)
        rows_in = jnp.repeat(mixed_in[first_row:first_row + group_rows], TOP, axis=0)
        rows_cot = slot_cot[first_row:first_row + group_rows].reshape(-1, D)
        buffer_in = jnp.zeros((EXPERTS * span, D), jnp.bfloat16).at[slot_place].set(rows_in).reshape(EXPERTS, span, D)
        buffer_cot = jnp.zeros((EXPERTS * span, D), jnp.bfloat16).at[slot_place].set(rows_cot).reshape(EXPERTS, span, D)
        outputs, d_inputs, grad_up_part, grad_down_part = lax.map(expert_pass, (buffer_in, buffer_cot, w_up, w_down))
        grad_up_part = lax.optimization_barrier(grad_up_part)
        grad_down_part = lax.optimization_barrier(grad_down_part)
        up_total = up_total + grad_up_part.astype(jnp.float32)
        down_total = down_total + grad_down_part.astype(jnp.float32)
        out_blocks.append(outputs.reshape(-1, D)[slot_place].reshape(group_rows, TOP, D))
        grad_blocks.append(d_inputs.reshape(-1, D)[slot_place].reshape(group_rows, TOP, D))
    expert_out = jnp.concatenate(out_blocks, axis=0)
    slot_grad = jnp.concatenate(grad_blocks, axis=0)
    layer_out = (mixed_in.astype(jnp.float32) + jnp.sum(gates[:, :, None] * expert_out.astype(jnp.float32), axis=1)).astype(jnp.bfloat16)
    d_gates = jnp.sum(expert_out.astype(jnp.float32) * cot_wide[:, None, :], axis=2)
    mean_term = jnp.sum(gates * d_gates, axis=1, keepdims=True)
    d_chosen = (d_gates - mean_term) / gate_total * squashed * (1.0 - squashed)
    route_hot = routes[:, :, None] == expert_ids[None, None, :]
    d_logits = jnp.sum(jnp.where(route_hot, d_chosen[:, :, None], 0.0), axis=1)
    d_router = jnp.dot(d_logits, router.astype(jnp.float32).T, precision=lax.Precision.HIGHEST)
    grad_in = (cot_wide + jnp.sum(slot_grad.astype(jnp.float32), axis=1) + d_router).astype(jnp.bfloat16)
    return layer_out, grad_in, up_total.astype(jnp.bfloat16), down_total.astype(jnp.bfloat16)
```

```python
import functools

import jax
import jax.numpy as jnp
from jax import lax
from jax.experimental import pallas as pl
from jax.experimental.pallas import tpu as pltpu
from jax.sharding import PartitionSpec as P

coef_a = 0.7978845608028654
coef_b = 0.044715
MESH = pl.DeviceIdType.MESH
F32, BF16 = jnp.float32, jnp.bfloat16
EXACT = lax.Precision.HIGHEST


def gelu_pair(pre_act):
    square = pre_act * pre_act
    tanh_val = jnp.tanh(coef_a * pre_act * (1.0 + coef_b * square))
    half = 0.5 * (1.0 + tanh_val)
    slope = half + 0.5 * pre_act * (1.0 - tanh_val * tanh_val) * (
        coef_a * (1.0 + 3.0 * coef_b * square)
    )
    return pre_act * half, slope


def dot(left, right, dims, precision=None):
    return lax.dot_general(
        left, right, ((dims[:1], dims[1:]), ((), ())),
        precision=precision, preferred_element_type=F32,
    )


def kernel(
    sizes,
    features, slots, routes, cotangent, pos_table, tower_in, tower_out, router, w_up, w_down,
    layer_out, grad_in, grad_up, grad_down,
    mixed_s, place_s, gate_s, squash_s,
    send_in, send_cot, recv_in, recv_cot, hid, slope, outs, d_acc, d_ins, back_out, back_grad,
    part_up, part_down, one_up, one_down, two_up, two_down,
    ex_send, ex_recv, ar_send, ar_recv,
):
    n_exp, cap, tiles = sizes
    tok, width = features.shape
    hidden = w_up.shape[1]
    step = hidden // tiles
    dp, me = lax.axis_index("dp"), lax.axis_index("expert")
    xb, yb = dp % 2, dp // 2
    x_peer, y_peer = dp + 1 - 2 * xb, dp + 2 - 4 * yb

    barrier = pltpu.get_barrier_semaphore()

    @pl.loop(1, n_exp)
    def _(d):
        pl.semaphore_signal(barrier, inc=1, device_id=(dp, (me + d) % n_exp), device_id_type=MESH)

    for peer in (x_peer, y_peer):
        pl.semaphore_signal(barrier, inc=1, device_id=(peer, me), device_id_type=MESH)

    pos_hidden = jnp.maximum(dot(pos_table[...], tower_in[...], (1, 0)), 0.0)
    pos_rows = dot(pos_hidden, tower_out[...].astype(F32), (1, 0), EXACT)
    n_pos = pos_table.shape[0]
    slot_hot = (slots[...] == lax.broadcasted_iota(jnp.int32, (tok, n_pos), 1)).astype(F32)
    pos_feats = dot(slot_hot, pos_rows, (1, 0), EXACT)
    mixed = (features[...].astype(F32) + pos_feats).astype(BF16)
    mixed_s[...] = mixed
    logits = dot(mixed, router[...], (1, 0))
    expert_ids = lax.broadcasted_iota(jnp.int32, (tok, n_exp), 1)
    hots = [(routes[:, k : k + 1] == expert_ids).astype(F32) for k in range(2)]
    earlier = (
        lax.broadcasted_iota(jnp.int32, (tok, tok), 1)
        < lax.broadcasted_iota(jnp.int32, (tok, tok), 0)
    ).astype(F32)
    before = dot(earlier.astype(BF16), (hots[0] + hots[1]).astype(BF16), (1, 0))
    squashed = [
        1.0 / (1.0 + jnp.exp(-jnp.sum(hot * logits, axis=1, keepdims=True))) for hot in hots
    ]
    total = squashed[0] + squashed[1]
    gates = [s / total for s in squashed]
    cot_wide = cotangent[...].astype(F32)
    cells = lax.broadcasted_iota(jnp.int32, (tok, n_exp * cap), 1)
    picks = []
    for k in range(2):
        rank = jnp.sum(hots[k] * before, axis=1, keepdims=True).astype(jnp.int32)
        place = routes[:, k : k + 1] * cap + rank
        place_s[:, k : k + 1] = place
        gate_s[:, k : k + 1] = gates[k]
        squash_s[:, k : k + 1] = squashed[k]
        picks.append((place == cells).astype(F32).astype(BF16))
    send_in[...] = dot(picks[0] + picks[1], mixed, (0, 0)).astype(BF16)

    pl.semaphore_wait(barrier, n_exp + 1)

    def exchange(number, source, target, d):
        peer = (me + d) % n_exp
        return pltpu.make_async_remote_copy(
            src_ref=source.at[pl.ds(pl.multiple_of(peer * cap, cap), cap)],
            dst_ref=target.at[pl.ds(pl.multiple_of(me * cap, cap), cap)],
            send_sem=ex_send.at[number, d],
            recv_sem=ex_recv.at[number, d],
            device_id=(dp, peer),
            device_id_type=MESH,
        )

    def start_exchange(number, source, target):
        @pl.loop(1, n_exp)
        def _(d):
            exchange(number, source, target, d).start()

        own = pl.ds(pl.multiple_of(me * cap, cap), cap)
        target[own, :] = source[own, :]

    def arrived(number, target):
        @pl.loop(1, n_exp)
        def _(d):
            giver = (me - d + n_exp) % n_exp
            rows = pl.ds(pl.multiple_of(giver * cap, cap), cap)
            pltpu.make_async_remote_copy(
                src_ref=target.at[rows],
                dst_ref=target.at[rows],
                send_sem=ex_send.at[number, d],
                recv_sem=ex_recv.at[number, d],
                device_id=(dp, (me + d) % n_exp),
                device_id_type=MESH,
            ).wait_recv()

    def sent(number, source, target):
        @pl.loop(1, n_exp)
        def _(d):
            exchange(number, source, target, d).wait_send()

    start_exchange(0, send_in, recv_in)
    cots = [(g * cot_wide).astype(BF16) for g in gates]
    send_cot[...] = (dot(picks[0], cots[0], (0, 0)) + dot(picks[1], cots[1], (0, 0))).astype(BF16)
    start_exchange(1, send_cot, recv_cot)
    arrived(0, recv_in)

    @pl.loop(0, tiles)
    def _(t):
        cols = pl.ds(pl.multiple_of(t * step, step), step)
        act, der = gelu_pair(dot(recv_in[...], w_up[:, cols], (1, 0)))
        act = act.astype(BF16)
        hid[t] = act
        slope[t] = der
        term = dot(act, w_down[cols, :], (1, 0))

        @pl.when(t == 0)
        def _():
            d_acc[...] = term

        @pl.when(t > 0)
        def _():
            d_acc[...] += term

    outs[...] = d_acc[...].astype(BF16)
    arrived(1, recv_cot)
    start_exchange(2, outs, back_out)

    half_u, half_d = width // 2, step // 2
    quart_u, quart_d = width // 4, step // 4

    def rows_of(big, index, size, small=None, inner=0):
        at = big + index * size
        if small is not None:
            at = at + inner * small
        return pl.multiple_of(at, small or size)

    def reduce_copy(phase, which, t):
        cols = pl.ds(pl.multiple_of(t * step, step), step)
        if which == 0:
            a, b = xb, yb
            first, second = (x_peer, me), (y_peer, me)
            base, half, quart = 0, half_u, quart_u
            part, one, two, final = part_up, one_up, two_up, grad_up
        else:
            a, b = yb, xb
            first, second = (y_peer, me), (x_peer, me)
            base, half, quart = t * step, half_d, quart_d
            part, one, two, final = part_down, one_down, two_down, grad_down

        def view(ref, start, size):
            rows = pl.ds(start, size)
            return ref.at[rows, cols] if which == 0 else ref.at[rows]

        if phase == 0:
            src, dst, peer = view(part, rows_of(base, 1 - a, half), half), one.at[t], first
        elif phase == 1:
            src = view(part, rows_of(base, a, half, quart, 1 - b), quart)
            dst, peer = two.at[t], second
        elif phase == 2:
            src = dst = view(final, rows_of(base, a, half, quart, b), quart)
            peer = second
        else:
            src = dst = view(final, rows_of(base, a, half), half)
            peer = first
        return pltpu.make_async_remote_copy(
            src_ref=src, dst_ref=dst,
            send_sem=ar_send.at[phase, which, t], recv_sem=ar_recv.at[phase, which, t],
            device_id=peer, device_id_type=MESH,
        )

    @pl.loop(0, tiles)
    def _(t):
        cols = pl.ds(pl.multiple_of(t * step, step), step)
        d_hidden = dot(recv_cot[...], w_down[cols, :], (1, 1))
        part_down[cols, :] = dot(hid[t], recv_cot[...], (0, 0)).astype(BF16)
        reduce_copy(0, 1, t).start()
        d_pre = (d_hidden * slope[t]).astype(BF16)
        part_up[:, cols] = dot(recv_in[...], d_pre, (0, 0)).astype(BF16)
        reduce_copy(0, 0, t).start()
        term = dot(d_pre, w_up[:, cols], (1, 1))

        @pl.when(t == 0)
        def _():
            d_acc[...] = term

        @pl.when(t > 0)
        def _():
            d_acc[...] += term

    d_ins[...] = d_acc[...].astype(BF16)
    start_exchange(3, d_ins, back_grad)

    @pl.loop(0, tiles)
    def _(t):
        cols = pl.ds(pl.multiple_of(t * step, step), step)
        reduce_copy(0, 1, t).wait_recv()
        rows = pl.ds(rows_of(t * step, yb, half_d), half_d)
        part_down[rows, :] = (part_down[rows, :].astype(F32) + one_down[t].astype(F32)).astype(BF16)
        reduce_copy(1, 1, t).start()
        reduce_copy(0, 0, t).wait_recv()
        rows = pl.ds(rows_of(0, xb, half_u), half_u)
        part_up[rows, cols] = (part_up[rows, cols].astype(F32) + one_up[t].astype(F32)).astype(BF16)
        reduce_copy(1, 0, t).start()

    @pl.loop(0, tiles)
    def _(t):
        cols = pl.ds(pl.multiple_of(t * step, step), step)
        reduce_copy(1, 1, t).wait_recv()
        rows = pl.ds(rows_of(t * step, yb, half_d, quart_d, xb), quart_d)
        grad_down[rows, :] = (part_down[rows, :].astype(F32) + two_down[t].astype(F32)).astype(BF16)
        reduce_copy(2, 1, t).start()
        reduce_copy(1, 0, t).wait_recv()
        rows = pl.ds(rows_of(0, xb, half_u, quart_u, yb), quart_u)
        grad_up[rows, cols] = (part_up[rows, cols].astype(F32) + two_up[t].astype(F32)).astype(BF16)
        reduce_copy(2, 0, t).start()

    def gathered(phase, which, t):
        cols = pl.ds(pl.multiple_of(t * step, step), step)
        a, b = (xb, yb) if which == 0 else (yb, xb)
        base, half, quart = (0, half_u, quart_u) if which == 0 else (t * step, half_d, quart_d)
        if phase == 2:
            rows = pl.ds(rows_of(base, a, half, quart, 1 - b), quart)
        else:
            rows = pl.ds(rows_of(base, 1 - a, half), half)
        ref = grad_up.at[rows, cols] if which == 0 else grad_down.at[rows]
        pltpu.make_async_remote_copy(
            src_ref=ref, dst_ref=ref,
            send_sem=ar_send.at[phase, which, t], recv_sem=ar_recv.at[phase, which, t],
            device_id=(x_peer, me), device_id_type=MESH,
        ).wait_recv()

    @pl.loop(0, tiles)
    def _(t):
        for which in (1, 0):
            gathered(2, which, t)
            reduce_copy(3, which, t).start()

    arrived(2, back_out)
    arrived(3, back_grad)
    cells = lax.broadcasted_iota(jnp.int32, (tok, n_exp * cap), 1)
    picks = [(place_s[:, k : k + 1] == cells).astype(F32).astype(BF16) for k in range(2)]
    gates = [gate_s[:, k : k + 1] for k in range(2)]
    squashed = [squash_s[:, k : k + 1] for k in range(2)]
    total = squashed[0] + squashed[1]
    cot_wide = cotangent[...].astype(F32)
    expert_out = [dot(pick, back_out[...], (1, 0)) for pick in picks]
    layer_out[...] = (
        mixed_s[...].astype(F32) + (gates[0] * expert_out[0] + gates[1] * expert_out[1])
    ).astype(BF16)
    d_gates = [jnp.sum(o * cot_wide, axis=1, keepdims=True) for o in expert_out]
    mean_term = gates[0] * d_gates[0] + gates[1] * d_gates[1]
    expert_ids = lax.broadcasted_iota(jnp.int32, (tok, n_exp), 1)
    d_logits = jnp.zeros((tok, n_exp), F32)
    for k in range(2):
        d_chosen = (d_gates[k] - mean_term) / total * squashed[k] * (1.0 - squashed[k])
        d_logits += jnp.where(routes[:, k : k + 1] == expert_ids, d_chosen, 0.0)
    d_router = dot(d_logits, router[...].astype(F32), (1, 1), EXACT)
    slot_sum = dot(picks[0] + picks[1], back_grad[...], (1, 0))
    grad_in[...] = (cot_wide + slot_sum + d_router).astype(BF16)

    sent(0, send_in, recv_in)
    sent(1, send_cot, recv_cot)
    sent(2, outs, back_out)
    sent(3, d_ins, back_grad)

    @pl.loop(0, tiles)
    def _(t):
        for which in (1, 0):
            gathered(3, which, t)
            for phase in range(4):
                reduce_copy(phase, which, t).wait_send()


def per_device(
    features, slots, routes, cotangent, pos_table, tower_in, tower_out, router, w_up, w_down
):
    tok, width = features.shape
    n_exp = router.shape[1]
    hidden = w_up.shape[2]
    cap = 4 * tok // n_exp
    rows = n_exp * cap
    tiles = 8
    step = hidden // tiles
    vmem = pl.BlockSpec(memory_space=pltpu.VMEM)
    dma = pltpu.SemaphoreType.DMA
    outs = pl.pallas_call(
        functools.partial(kernel, (n_exp, cap, tiles)),
        out_shape=(
            jax.ShapeDtypeStruct((tok, width), BF16),
            jax.ShapeDtypeStruct((tok, width), BF16),
            jax.ShapeDtypeStruct((width, hidden), BF16),
            jax.ShapeDtypeStruct((hidden, width), BF16),
        ),
        in_specs=[vmem] * 10,
        out_specs=(vmem,) * 4,
        scratch_shapes=[
            pltpu.VMEM((tok, width), BF16),
            pltpu.VMEM((tok, 2), jnp.int32),
            pltpu.VMEM((tok, 2), F32),
            pltpu.VMEM((tok, 2), F32),
            pltpu.VMEM((rows, width), BF16),
            pltpu.VMEM((rows, width), BF16),
            pltpu.VMEM((rows, width), BF16),
            pltpu.VMEM((rows, width), BF16),
            pltpu.VMEM((tiles, rows, step), BF16),
            pltpu.VMEM((tiles, rows, step), F32),
            pltpu.VMEM((rows, width), BF16),
            pltpu.VMEM((rows, width), F32),
            pltpu.VMEM((rows, width), BF16),
            pltpu.VMEM((rows, width), BF16),
            pltpu.VMEM((rows, width), BF16),
            pltpu.VMEM((width, hidden), BF16),
            pltpu.VMEM((hidden, width), BF16),
            pltpu.VMEM((tiles, width // 2, step), BF16),
            pltpu.VMEM((tiles, step // 2, width), BF16),
            pltpu.VMEM((tiles, width // 4, step), BF16),
            pltpu.VMEM((tiles, step // 4, width), BF16),
            dma((4, n_exp)),
            dma((4, n_exp)),
            dma((4, 2, tiles)),
            dma((4, 2, tiles)),
        ],
        compiler_params=pltpu.CompilerParams(
            collective_id=0, has_side_effects=True, vmem_limit_bytes=60 * 1024 * 1024
        ),
    )(
        features, slots[:, None], routes, cotangent, pos_table, tower_in, tower_out, router,
        w_up[0], w_down[0],
    )
    return outs[0], outs[1], outs[2][None], outs[3][None]


def solution(mesh):
    return jax.shard_map(
        per_device,
        mesh=mesh,
        in_specs=(
            P(("dp", "expert"), None),
            P(("dp", "expert")),
            P(("dp", "expert"), None),
            P(("dp", "expert"), None),
            P(),
            P(),
            P(),
            P(),
            P("expert", None, None),
            P("expert", None, None),
        ),
        out_specs=(
            P(("dp", "expert"), None),
            P(("dp", "expert"), None),
            P("expert", None, None),
            P("expert", None, None),
        ),
        check_vma=False,
    )
```

```python
import functools

import jax
import jax.numpy as jnp
from jax import lax
from jax.experimental import pallas as pl
from jax.experimental.pallas import tpu as pltpu
from jax.sharding import PartitionSpec as P

coef_a = 0.7978845608028654
coef_b = 0.044715
MESH = pl.DeviceIdType.MESH
F32, BF16 = jnp.float32, jnp.bfloat16
EXACT = lax.Precision.HIGHEST


def gelu_pair(pre_act):
    square = pre_act * pre_act
    tanh_val = jnp.tanh(coef_a * pre_act * (1.0 + coef_b * square))
    half = 0.5 * (1.0 + tanh_val)
    slope = half + 0.5 * pre_act * (1.0 - tanh_val * tanh_val) * (
        coef_a * (1.0 + 3.0 * coef_b * square)
    )
    return pre_act * half, slope


def dot(left, right, dims, precision=None):
    return lax.dot_general(
        left, right, ((dims[:1], dims[1:]), ((), ())),
        precision=precision, preferred_element_type=F32,
    )


def kernel(
    sizes,
    features, slots, routes, cotangent, pos_table, tower_in, tower_out, router, w_up, w_down,
    layer_out, grad_in, grad_up, grad_down,
    mixed_s, place_s, route_s, gate_s, squash_s,
    send_in, send_cot, recv_in, recv_cot, hid, slope, outs, d_acc, d_ins, back_out, back_grad,
    part_up, part_down, one_up, one_down, two_up, two_down,
    ex_send, ex_recv, ar_send, ar_recv, *near,
):
    n_exp, cap, tiles = sizes
    tok, width = features.shape
    hidden = w_up.shape[1]
    step = hidden // tiles
    dp, me = lax.axis_index("dp"), lax.axis_index("expert")
    xb, yb = dp % 2, dp // 2
    x_peer, y_peer = dp + 1 - 2 * xb, dp + 2 - 4 * yb

    barrier = pltpu.get_barrier_semaphore()

    @pl.loop(1, n_exp)
    def _(d):
        pl.semaphore_signal(barrier, inc=1, device_id=(dp, (me + d) % n_exp), device_id_type=MESH)

    for peer in (x_peer, y_peer):
        pl.semaphore_signal(barrier, inc=1, device_id=(peer, me), device_id_type=MESH)

    pl.semaphore_wait(barrier, n_exp + 1)

    if near:
        all_in, all_cot, send_meta, recv_meta, go_send, go_recv = near
        alls = (all_in, all_cot)
        chips = n_exp // 2
        z, core = me // 2, me % 2
        twin = me + 1 - 2 * core

    def passing(a, chip, way, number):
        item = alls[a].at[2 * chip + core]
        return pltpu.make_async_remote_copy(
            src_ref=item, dst_ref=item,
            send_sem=go_send.at[a, way, number], recv_sem=go_recv.at[a, 2 * chip + core],
            device_id=(dp, (me + 2, me - 2, twin)[way]), device_id_type=MESH,
        )

    def landed(a, device):
        item = alls[a].at[device]
        pltpu.make_async_remote_copy(
            src_ref=item, dst_ref=item,
            send_sem=go_send.at[a, 0, 0], recv_sem=go_recv.at[a, device],
            device_id=(dp, twin), device_id_type=MESH,
        ).wait_recv()

    def onward(a, chip, way, number):
        @pl.when(z < chips - 1 if way == 0 else z > 0)
        def _():
            passing(a, chip, way, number).start()

    def pass_first(a):
        onward(a, z, 0, 0)
        onward(a, z, 1, 0)
        passing(a, z, 2, z).start()

    def pass_on(a, j):
        for way, chip, there in ((0, z - 1 - j, z - 1 - j >= 0), (1, z + 1 + j, z + 1 + j < chips)):
            @pl.when(there)
            def _():
                landed(a, 2 * chip + core)
                onward(a, chip, way, j + 1)
                passing(a, chip, 2, chip).start()

    def pass_last(a):
        @pl.loop(0, chips)
        def _(chip):
            landed(a, 2 * chip + 1 - core)

    def passed(a):
        for j in range(chips - 1):
            for way, chip, there in ((0, z - j, (z - j >= 0) & (z < chips - 1)),
                                     (1, z + j, (z + j < chips) & (z > 0))):
                @pl.when(there)
                def _():
                    passing(a, chip, way, j).wait_send()

        @pl.loop(0, chips)
        def _(chip):
            passing(a, chip, 2, chip).wait_send()

    if near:
        all_cot[me] = cotangent[...]
        pass_first(1)

    diagonal = lax.broadcasted_iota(jnp.int32, (tok, tok), 0) == lax.broadcasted_iota(
        jnp.int32, (tok, tok), 1
    )
    diagonal = diagonal.astype(F32)
    slot_col, first_col, second_col = [
        jnp.sum(diagonal * row.astype(F32), axis=1, keepdims=True)
        for row in (slots[...], routes[0:1, :], routes[1:2, :])
    ]
    route_cols = (first_col, second_col)
    pos_hidden = jnp.maximum(dot(pos_table[...], tower_in[...], (1, 0)), 0.0)
    pos_rows = dot(pos_hidden, tower_out[...].astype(F32), (1, 0), EXACT)

    def count(shape, dim):
        return lax.broadcasted_iota(jnp.int32, shape, dim).astype(F32)

    slot_hot = (slot_col == count((tok, pos_table.shape[0]), 1)).astype(F32)
    pos_feats = dot(slot_hot, pos_rows, (1, 0), EXACT)
    mixed = (features[...].astype(F32) + pos_feats).astype(BF16)
    mixed_s[...] = mixed
    if near:
        all_in[me] = mixed
        pass_first(0)
    logits = dot(mixed, router[...], (1, 1))
    hots = [
        (route_cols[k] == count((tok, n_exp), 1)).astype(F32) for k in range(2)
    ]
    earlier = (count((tok, tok), 1) < count((tok, tok), 0)).astype(F32)
    both = hots[0] + hots[1]
    before = dot(earlier.astype(BF16), both.astype(BF16), (1, 0))
    squashed = [
        1.0 / (1.0 + jnp.exp(-jnp.sum(hot * logits, axis=1, keepdims=True))) for hot in hots
    ]
    total = squashed[0] + squashed[1]
    gates = [s / total for s in squashed]
    for k in range(2):
        rank = jnp.sum(hots[k] * before, axis=1, keepdims=True)
        place_s[:, k : k + 1] = route_cols[k] * cap + rank
        route_s[:, k : k + 1] = route_cols[k]
        gate_s[:, k : k + 1] = gates[k]
        squash_s[:, k : k + 1] = squashed[k]

    def picks_of():
        cells = count((tok, n_exp * cap), 1)
        return [(place_s[:, k : k + 1] == cells).astype(F32).astype(BF16) for k in range(2)]

    def exchange(number, source, target, d):
        size = source.shape[0] // n_exp
        peer = (me + d) % n_exp
        return pltpu.make_async_remote_copy(
            src_ref=source.at[pl.ds(pl.multiple_of(peer * size, size), size)],
            dst_ref=target.at[pl.ds(pl.multiple_of(me * size, size), size)],
            send_sem=ex_send.at[number, d],
            recv_sem=ex_recv.at[number, d],
            device_id=(dp, peer),
            device_id_type=MESH,
        )

    def start_exchange(number, source, target):
        @pl.loop(1, n_exp)
        def _(d):
            exchange(number, source, target, d).start()

        size = source.shape[0] // n_exp
        own = pl.ds(pl.multiple_of(me * size, size), size)
        target[own, :] = source[own, :]

    def arrived(number, target):
        @pl.loop(1, n_exp)
        def _(d):
            giver = (me - d + n_exp) % n_exp
            size = target.shape[0] // n_exp
            rows = pl.ds(pl.multiple_of(giver * size, size), size)
            pltpu.make_async_remote_copy(
                src_ref=target.at[rows],
                dst_ref=target.at[rows],
                send_sem=ex_send.at[number, d],
                recv_sem=ex_recv.at[number, d],
                device_id=(dp, (me + d) % n_exp),
                device_id_type=MESH,
            ).wait_recv()

    def sent(number, source, target):
        @pl.loop(1, n_exp)
        def _(d):
            exchange(number, source, target, d).wait_send()

    if near:
        ranks = (both * (before + 1.0) - 1.0).astype(BF16)
        rank_rows = dot(ranks, diagonal.astype(BF16), (0, 0))
        gate_rows = dot(hots[0] * gates[0] + hots[1] * gates[1], diagonal, (0, 0), EXACT)
        send_meta[...] = jnp.zeros_like(send_meta)
        for e in range(n_exp):
            send_meta[8 * e : 8 * e + 1, :] = rank_rows[e : e + 1]
            send_meta[8 * e + 1 : 8 * e + 2, :] = gate_rows[e : e + 1]
        start_exchange(0, send_meta, recv_meta)
        for j in range(chips - 1):
            pass_on(0, j)
            if j == chips - 3:
                pass_on(1, 0)
        pass_last(0)
        arrived(0, recv_meta)

        def choice(s):
            rank = recv_meta[pl.ds(pl.multiple_of(8 * s, 8), 8), :][0:1, :]
            return rank == count((cap, tok), 0)

        @pl.loop(0, n_exp)
        def _(s):
            rows = pl.ds(pl.multiple_of(s * cap, cap), cap)
            recv_in[rows, :] = dot(choice(s).astype(F32).astype(BF16), all_in[s], (1, 0)).astype(BF16)
    else:
        picks = picks_of()
        send_in[...] = dot(picks[0] + picks[1], mixed, (0, 0)).astype(BF16)
        start_exchange(0, send_in, recv_in)
        cot_wide = cotangent[...].astype(F32)
        cots = [(g * cot_wide).astype(BF16) for g in gates]
        send_cot[...] = (
            dot(picks[0], cots[0], (0, 0)) + dot(picks[1], cots[1], (0, 0))
        ).astype(BF16)
        start_exchange(1, send_cot, recv_cot)
        arrived(0, recv_in)

    def forward(t):
        cols = pl.ds(pl.multiple_of(t * step, step), step)
        act, der = gelu_pair(dot(recv_in[...], w_up[:, cols], (1, 0)))
        act = act.astype(BF16)
        hid[t] = act
        slope[t] = der
        term = dot(act, w_down[cols, :], (1, 0))

        @pl.when(t == 0)
        def _():
            d_acc[...] = term

        @pl.when(t > 0)
        def _():
            d_acc[...] += term

    if near:
        bounds = [tiles * j // chips for j in range(chips)] + [tiles]
        pl.loop(0, bounds[1])(forward)
        for j in range(1, chips - 1):
            pass_on(1, j)
            pl.loop(bounds[j], bounds[j + 1])(forward)
        pl.loop(bounds[chips - 1], tiles)(forward)
        pass_last(1)

        @pl.loop(0, n_exp)
        def _(s):
            rows = pl.ds(pl.multiple_of(s * cap, cap), cap)
            chosen = choice(s)
            gate = recv_meta[pl.ds(pl.multiple_of(8 * s, 8), 8), :][1:2, :]
            gate = jnp.sum(jnp.where(chosen, gate, 0.0), axis=1, keepdims=True)
            picked = dot(chosen.astype(F32).astype(BF16), all_cot[s], (1, 0))
            recv_cot[rows, :] = (gate * picked).astype(BF16)
    else:
        pl.loop(0, tiles)(forward)
        arrived(1, recv_cot)
    outs[...] = d_acc[...].astype(BF16)
    start_exchange(2, outs, back_out)

    half_u, half_d = width // 2, step // 2
    quart_u, quart_d = width // 4, step // 4

    def rows_of(big, index, size, small=None, inner=0):
        at = big + index * size
        if small is not None:
            at = at + inner * small
        return pl.multiple_of(at, small or size)

    def reduce_copy(phase, which, t):
        cols = pl.ds(pl.multiple_of(t * step, step), step)
        if which == 0:
            a, b = xb, yb
            first, second = (x_peer, me), (y_peer, me)
            base, half, quart = 0, half_u, quart_u
            part, one, two, final = part_up, one_up, two_up, grad_up
        else:
            a, b = yb, xb
            first, second = (y_peer, me), (x_peer, me)
            base, half, quart = t * step, half_d, quart_d
            part, one, two, final = part_down, one_down, two_down, grad_down

        def view(ref, start, size):
            rows = pl.ds(start, size)
            return ref.at[rows, cols] if which == 0 else ref.at[rows]

        if phase == 0:
            src, dst, peer = view(part, rows_of(base, 1 - a, half), half), one.at[t], first
        elif phase == 1:
            src = view(part, rows_of(base, a, half, quart, 1 - b), quart)
            dst, peer = two.at[t], second
        elif phase == 2:
            src = dst = view(final, rows_of(base, a, half, quart, b), quart)
            peer = second
        else:
            src = dst = view(final, rows_of(base, a, half), half)
            peer = first
        return pltpu.make_async_remote_copy(
            src_ref=src, dst_ref=dst,
            send_sem=ar_send.at[phase, which, t], recv_sem=ar_recv.at[phase, which, t],
            device_id=peer, device_id_type=MESH,
        )

    @pl.loop(0, tiles)
    def _(t):
        cols = pl.ds(pl.multiple_of(t * step, step), step)
        d_hidden = dot(recv_cot[...], w_down[cols, :], (1, 1))
        part_down[cols, :] = dot(hid[t], recv_cot[...], (0, 0)).astype(BF16)
        reduce_copy(0, 1, t).start()
        d_pre = (d_hidden * slope[t]).astype(BF16)
        part_up[:, cols] = dot(recv_in[...], d_pre, (0, 0)).astype(BF16)
        reduce_copy(0, 0, t).start()
        term = dot(d_pre, w_up[:, cols], (1, 1))

        @pl.when(t == 0)
        def _():
            d_acc[...] = term

        @pl.when(t > 0)
        def _():
            d_acc[...] += term

    d_ins[...] = d_acc[...].astype(BF16)
    start_exchange(3, d_ins, back_grad)

    @pl.loop(0, tiles)
    def _(t):
        cols = pl.ds(pl.multiple_of(t * step, step), step)
        reduce_copy(0, 1, t).wait_recv()
        rows = pl.ds(rows_of(t * step, yb, half_d), half_d)
        part_down[rows, :] = (part_down[rows, :].astype(F32) + one_down[t].astype(F32)).astype(BF16)
        reduce_copy(1, 1, t).start()
        reduce_copy(0, 0, t).wait_recv()
        rows = pl.ds(rows_of(0, xb, half_u), half_u)
        part_up[rows, cols] = (part_up[rows, cols].astype(F32) + one_up[t].astype(F32)).astype(BF16)
        reduce_copy(1, 0, t).start()

    @pl.loop(0, tiles)
    def _(t):
        cols = pl.ds(pl.multiple_of(t * step, step), step)
        reduce_copy(1, 1, t).wait_recv()
        rows = pl.ds(rows_of(t * step, yb, half_d, quart_d, xb), quart_d)
        grad_down[rows, :] = (part_down[rows, :].astype(F32) + two_down[t].astype(F32)).astype(BF16)
        reduce_copy(2, 1, t).start()
        reduce_copy(1, 0, t).wait_recv()
        rows = pl.ds(rows_of(0, xb, half_u, quart_u, yb), quart_u)
        grad_up[rows, cols] = (part_up[rows, cols].astype(F32) + two_up[t].astype(F32)).astype(BF16)
        reduce_copy(2, 0, t).start()

    def gathered(phase, which, t):
        cols = pl.ds(pl.multiple_of(t * step, step), step)
        a, b = (xb, yb) if which == 0 else (yb, xb)
        base, half, quart = (0, half_u, quart_u) if which == 0 else (t * step, half_d, quart_d)
        if phase == 2:
            rows = pl.ds(rows_of(base, a, half, quart, 1 - b), quart)
        else:
            rows = pl.ds(rows_of(base, 1 - a, half), half)
        ref = grad_up.at[rows, cols] if which == 0 else grad_down.at[rows]
        pltpu.make_async_remote_copy(
            src_ref=ref, dst_ref=ref,
            send_sem=ar_send.at[phase, which, t], recv_sem=ar_recv.at[phase, which, t],
            device_id=(x_peer, me), device_id_type=MESH,
        ).wait_recv()

    @pl.loop(0, tiles)
    def _(t):
        for which in (1, 0):
            gathered(2, which, t)
            reduce_copy(3, which, t).start()

    arrived(2, back_out)
    arrived(3, back_grad)
    picks = picks_of()
    gates = [gate_s[:, k : k + 1] for k in range(2)]
    squashed = [squash_s[:, k : k + 1] for k in range(2)]
    total = squashed[0] + squashed[1]
    cot_wide = cotangent[...].astype(F32)
    expert_out = [dot(pick, back_out[...], (1, 0)) for pick in picks]
    layer_out[...] = (
        mixed_s[...].astype(F32) + (gates[0] * expert_out[0] + gates[1] * expert_out[1])
    ).astype(BF16)
    d_gates = [jnp.sum(o * cot_wide, axis=1, keepdims=True) for o in expert_out]
    mean_term = gates[0] * d_gates[0] + gates[1] * d_gates[1]
    expert_ids = count((tok, n_exp), 1)
    d_logits = jnp.zeros((tok, n_exp), F32)
    for k in range(2):
        d_chosen = (d_gates[k] - mean_term) / total * squashed[k] * (1.0 - squashed[k])
        d_logits += jnp.where(route_s[:, k : k + 1] == expert_ids, d_chosen, 0.0)
    d_router = dot(d_logits, router[...].astype(F32), (1, 0), EXACT)
    slot_sum = dot(picks[0] + picks[1], back_grad[...], (1, 0))
    grad_in[...] = (cot_wide + slot_sum + d_router).astype(BF16)

    if near:
        sent(0, send_meta, recv_meta)
        passed(0)
        passed(1)
    else:
        sent(0, send_in, recv_in)
        sent(1, send_cot, recv_cot)
    sent(2, outs, back_out)
    sent(3, d_ins, back_grad)

    @pl.loop(0, tiles)
    def _(t):
        for which in (1, 0):
            gathered(3, which, t)
            for phase in range(4):
                reduce_copy(phase, which, t).wait_send()


def copy_out(*refs):
    sems = refs[8]
    copies = [pltpu.make_async_copy(refs[i], refs[4 + i], sems.at[i]) for i in range(4)]
    for copy in copies:
        copy.start()
    for copy in copies:
        copy.wait()


def per_device(
    features, slots, routes, cotangent, pos_table, tower_in, tower_out, router, w_up, w_down
):
    tok, width = features.shape
    n_exp = router.shape[1]
    hidden = w_up.shape[2]
    cap = 4 * tok // n_exp
    rows = n_exp * cap
    tiles = 8
    step = hidden // tiles
    vmem = pl.BlockSpec(memory_space=pltpu.VMEM)
    dma = pltpu.SemaphoreType.DMA
    near = []
    if n_exp == 8:
        near = [
            pltpu.VMEM((n_exp, tok, width), BF16),
            pltpu.VMEM((n_exp, tok, width), BF16),
            pltpu.VMEM((n_exp * 8, tok), F32),
            pltpu.VMEM((n_exp * 8, tok), F32),
            dma((2, 3, n_exp // 2)),
            dma((2, n_exp)),
        ]
    outs = pl.pallas_call(
        functools.partial(kernel, (n_exp, cap, tiles)),
        out_shape=(
            jax.ShapeDtypeStruct((tok, width), BF16),
            jax.ShapeDtypeStruct((tok, width), BF16),
            jax.ShapeDtypeStruct((width, hidden), BF16),
            jax.ShapeDtypeStruct((hidden, width), BF16),
        ),
        in_specs=[vmem] * 10,
        out_specs=(vmem,) * 4,
        scratch_shapes=[
            pltpu.VMEM((tok, width), BF16),
            pltpu.VMEM((tok, 2), F32),
            pltpu.VMEM((tok, 2), F32),
            pltpu.VMEM((tok, 2), F32),
            pltpu.VMEM((tok, 2), F32),
            pltpu.VMEM((rows, width), BF16),
            pltpu.VMEM((rows, width), BF16),
            pltpu.VMEM((rows, width), BF16),
            pltpu.VMEM((rows, width), BF16),
            pltpu.VMEM((tiles, rows, step), BF16),
            pltpu.VMEM((tiles, rows, step), F32),
            pltpu.VMEM((rows, width), BF16),
            pltpu.VMEM((rows, width), F32),
            pltpu.VMEM((rows, width), BF16),
            pltpu.VMEM((rows, width), BF16),
            pltpu.VMEM((rows, width), BF16),
            pltpu.VMEM((width, hidden), BF16),
            pltpu.VMEM((hidden, width), BF16),
            pltpu.VMEM((tiles, width // 2, step), BF16),
            pltpu.VMEM((tiles, step // 2, width), BF16),
            pltpu.VMEM((tiles, width // 4, step), BF16),
            pltpu.VMEM((tiles, step // 4, width), BF16),
            dma((4, n_exp)),
            dma((4, n_exp)),
            dma((4, 2, tiles)),
            dma((4, 2, tiles)),
        ]
        + near,
        compiler_params=pltpu.CompilerParams(
            collective_id=0, has_side_effects=True, vmem_limit_bytes=60 * 1024 * 1024
        ),
    )(
        features, slots[None], routes.T, cotangent, pos_table, tower_in, tower_out, router.T,
        w_up[0], w_down[0],
    )
    outs = pl.pallas_call(
        copy_out,
        out_shape=tuple(jax.ShapeDtypeStruct(o.shape, o.dtype) for o in outs),
        in_specs=[pl.BlockSpec(memory_space=pl.ANY)] * 4,
        out_specs=(pl.BlockSpec(memory_space=pl.ANY),) * 4,
        scratch_shapes=[dma((4,))],
    )(*outs)
    return outs[0], outs[1], outs[2][None], outs[3][None]


def solution(mesh):
    return jax.shard_map(
        per_device,
        mesh=mesh,
        in_specs=(
            P(("dp", "expert"), None),
            P(("dp", "expert")),
            P(("dp", "expert"), None),
            P(("dp", "expert"), None),
            P(),
            P(),
            P(),
            P(),
            P("expert", None, None),
            P("expert", None, None),
        ),
        out_specs=(
            P(("dp", "expert"), None),
            P(("dp", "expert"), None),
            P("expert", None, None),
            P("expert", None, None),
        ),
        check_vma=False,
    )
```

```python
import functools

import jax
import jax.numpy as jnp
from jax import lax
from jax.experimental import pallas as pl
from jax.experimental.pallas import tpu as pltpu
from jax.sharding import PartitionSpec as P

coef_a = 0.7978845608028654
coef_b = 0.044715
MESH = pl.DeviceIdType.MESH
F32, BF16 = jnp.float32, jnp.bfloat16
EXACT = lax.Precision.HIGHEST


def gelu_pair(pre_act):
    square = pre_act * pre_act
    tanh_val = jnp.tanh(coef_a * pre_act * (1.0 + coef_b * square))
    half = 0.5 * (1.0 + tanh_val)
    slope = half + 0.5 * pre_act * (1.0 - tanh_val * tanh_val) * (
        coef_a * (1.0 + 3.0 * coef_b * square)
    )
    return pre_act * half, slope


def dot(left, right, dims, precision=None):
    return lax.dot_general(
        left, right, ((dims[:1], dims[1:]), ((), ())),
        precision=precision, preferred_element_type=F32,
    )


def kernel(
    sizes,
    features, slots, routes, cotangent, pos_table, tower_in, tower_out, router, w_up, w_down,
    layer_out, grad_in, grad_up, grad_down,
    mixed_s, place_s, route_s, gate_s, squash_s,
    send_in, send_cot, recv_in, recv_cot, hid, slope, outs, d_acc, d_ins, back_out, back_grad,
    part_up, part_down, one_up, one_down, two_up, two_down,
    ex_send, ex_recv, ar_send, ar_recv, *near,
):
    n_exp, cap, tiles = sizes
    tok, width = features.shape
    hidden = w_up.shape[1]
    step = hidden // tiles
    dp, me = lax.axis_index("dp"), lax.axis_index("expert")
    xb, yb = dp % 2, dp // 2
    x_peer, y_peer = dp + 1 - 2 * xb, dp + 2 - 4 * yb

    barrier = pltpu.get_barrier_semaphore()

    @pl.loop(1, n_exp)
    def _(d):
        pl.semaphore_signal(barrier, inc=1, device_id=(dp, (me + d) % n_exp), device_id_type=MESH)

    for peer in (x_peer, y_peer):
        pl.semaphore_signal(barrier, inc=1, device_id=(peer, me), device_id_type=MESH)

    pl.semaphore_wait(barrier, n_exp + 1)

    if near:
        all_in, all_cot, send_meta, recv_meta, go_send, go_recv = near
        alls = (all_in, all_cot)
        chips = n_exp // 2
        z, core = me // 2, me % 2
        twin = me + 1 - 2 * core

    def passing(a, chip, way, number):
        item = alls[a].at[2 * chip + core]
        return pltpu.make_async_remote_copy(
            src_ref=item, dst_ref=item,
            send_sem=go_send.at[a, way, number], recv_sem=go_recv.at[a, 2 * chip + core],
            device_id=(dp, (me + 2, me - 2, twin)[way]), device_id_type=MESH,
        )

    def landed(a, device):
        item = alls[a].at[device]
        pltpu.make_async_remote_copy(
            src_ref=item, dst_ref=item,
            send_sem=go_send.at[a, 0, 0], recv_sem=go_recv.at[a, device],
            device_id=(dp, twin), device_id_type=MESH,
        ).wait_recv()

    def onward(a, chip, way, number):
        @pl.when(z < chips - 1 if way == 0 else z > 0)
        def _():
            passing(a, chip, way, number).start()

    def pass_first(a):
        onward(a, z, 0, 0)
        onward(a, z, 1, 0)
        passing(a, z, 2, z).start()

    def pass_on(a, j):
        for way, chip, there in ((0, z - 1 - j, z - 1 - j >= 0), (1, z + 1 + j, z + 1 + j < chips)):
            @pl.when(there)
            def _():
                landed(a, 2 * chip + core)
                onward(a, chip, way, j + 1)
                passing(a, chip, 2, chip).start()

    def pass_last(a):
        @pl.loop(0, chips)
        def _(chip):
            landed(a, 2 * chip + 1 - core)

    def passed(a):
        for j in range(chips - 1):
            for way, chip, there in ((0, z - j, (z - j >= 0) & (z < chips - 1)),
                                     (1, z + j, (z + j < chips) & (z > 0))):
                @pl.when(there)
                def _():
                    passing(a, chip, way, j).wait_send()

        @pl.loop(0, chips)
        def _(chip):
            passing(a, chip, 2, chip).wait_send()

    if near:
        all_cot[me] = cotangent[...]
        pass_first(1)

    diagonal = lax.broadcasted_iota(jnp.int32, (tok, tok), 0) == lax.broadcasted_iota(
        jnp.int32, (tok, tok), 1
    )
    diagonal = diagonal.astype(F32)
    slot_col, first_col, second_col = [
        jnp.sum(diagonal * row.astype(F32), axis=1, keepdims=True)
        for row in (slots[...], routes[0:1, :], routes[1:2, :])
    ]
    route_cols = (first_col, second_col)
    pos_hidden = jnp.maximum(dot(pos_table[...], tower_in[...], (1, 0)), 0.0)
    pos_rows = dot(pos_hidden, tower_out[...].astype(F32), (1, 0), EXACT)

    def count(shape, dim):
        return lax.broadcasted_iota(jnp.int32, shape, dim).astype(F32)

    slot_hot = (slot_col == count((tok, pos_table.shape[0]), 1)).astype(F32)
    pos_feats = dot(slot_hot, pos_rows, (1, 0), EXACT)
    mixed = (features[...].astype(F32) + pos_feats).astype(BF16)
    mixed_s[...] = mixed
    if near:
        all_in[me] = mixed
        pass_first(0)
    logits = dot(mixed, router[...], (1, 1))
    hots = [
        (route_cols[k] == count((tok, n_exp), 1)).astype(F32) for k in range(2)
    ]
    earlier = (count((tok, tok), 1) < count((tok, tok), 0)).astype(F32)
    both = hots[0] + hots[1]
    before = dot(earlier.astype(BF16), both.astype(BF16), (1, 0))
    squashed = [
        1.0 / (1.0 + jnp.exp(-jnp.sum(hot * logits, axis=1, keepdims=True))) for hot in hots
    ]
    total = squashed[0] + squashed[1]
    gates = [s / total for s in squashed]
    for k in range(2):
        rank = jnp.sum(hots[k] * before, axis=1, keepdims=True)
        place_s[:, k : k + 1] = route_cols[k] * cap + rank
        route_s[:, k : k + 1] = route_cols[k]
        gate_s[:, k : k + 1] = gates[k]
        squash_s[:, k : k + 1] = squashed[k]

    def picks_of():
        cells = count((tok, n_exp * cap), 1)
        return [(place_s[:, k : k + 1] == cells).astype(F32).astype(BF16) for k in range(2)]

    def exchange(number, source, target, d):
        size = source.shape[0] // n_exp
        peer = (me + d) % n_exp
        return pltpu.make_async_remote_copy(
            src_ref=source.at[pl.ds(pl.multiple_of(peer * size, size), size)],
            dst_ref=target.at[pl.ds(pl.multiple_of(me * size, size), size)],
            send_sem=ex_send.at[number, d],
            recv_sem=ex_recv.at[number, d],
            device_id=(dp, peer),
            device_id_type=MESH,
        )

    def start_exchange(number, source, target):
        @pl.loop(1, n_exp)
        def _(d):
            exchange(number, source, target, d).start()

        size = source.shape[0] // n_exp
        own = pl.ds(pl.multiple_of(me * size, size), size)
        target[own, :] = source[own, :]

    def arrived(number, target):
        @pl.loop(1, n_exp)
        def _(d):
            giver = (me - d + n_exp) % n_exp
            size = target.shape[0] // n_exp
            rows = pl.ds(pl.multiple_of(giver * size, size), size)
            pltpu.make_async_remote_copy(
                src_ref=target.at[rows],
                dst_ref=target.at[rows],
                send_sem=ex_send.at[number, d],
                recv_sem=ex_recv.at[number, d],
                device_id=(dp, (me + d) % n_exp),
                device_id_type=MESH,
            ).wait_recv()

    def sent(number, source, target):
        @pl.loop(1, n_exp)
        def _(d):
            exchange(number, source, target, d).wait_send()

    if near:
        ranks = (both * (before + 1.0) - 1.0).astype(BF16)
        rank_rows = dot(ranks, diagonal.astype(BF16), (0, 0))
        gate_rows = dot(hots[0] * gates[0] + hots[1] * gates[1], diagonal, (0, 0), EXACT)
        send_meta[...] = jnp.zeros_like(send_meta)
        for e in range(n_exp):
            send_meta[8 * e : 8 * e + 1, :] = rank_rows[e : e + 1]
            send_meta[8 * e + 1 : 8 * e + 2, :] = gate_rows[e : e + 1]
        start_exchange(0, send_meta, recv_meta)
        for j in range(chips - 1):
            pass_on(0, j)
            if j == chips - 3:
                pass_on(1, 0)
        pass_last(0)
        arrived(0, recv_meta)

        def choice(s):
            rank = recv_meta[pl.ds(pl.multiple_of(8 * s, 8), 8), :][0:1, :]
            return rank == count((cap, tok), 0)

        @pl.loop(0, n_exp)
        def _(s):
            rows = pl.ds(pl.multiple_of(s * cap, cap), cap)
            recv_in[rows, :] = dot(choice(s).astype(F32).astype(BF16), all_in[s], (1, 0)).astype(BF16)
    else:
        picks = picks_of()
        send_in[...] = dot(picks[0] + picks[1], mixed, (0, 0)).astype(BF16)
        start_exchange(0, send_in, recv_in)
        cot_wide = cotangent[...].astype(F32)
        cots = [(g * cot_wide).astype(BF16) for g in gates]
        send_cot[...] = (
            dot(picks[0], cots[0], (0, 0)) + dot(picks[1], cots[1], (0, 0))
        ).astype(BF16)
        start_exchange(1, send_cot, recv_cot)
        arrived(0, recv_in)

    def forward(t):
        cols = pl.ds(pl.multiple_of(t * step, step), step)
        act, der = gelu_pair(dot(recv_in[...], w_up[:, cols], (1, 0)))
        act = act.astype(BF16)
        hid[t] = act
        slope[t] = der
        term = dot(act, w_down[cols, :], (1, 0))

        @pl.when(t == 0)
        def _():
            d_acc[...] = term

        @pl.when(t > 0)
        def _():
            d_acc[...] += term

    if near:
        bounds = [tiles * j // chips for j in range(chips)] + [tiles]
        pl.loop(0, bounds[1])(forward)
        for j in range(1, chips - 1):
            pass_on(1, j)
            pl.loop(bounds[j], bounds[j + 1])(forward)
        pl.loop(bounds[chips - 1], tiles)(forward)
        pass_last(1)

        @pl.loop(0, n_exp)
        def _(s):
            rows = pl.ds(pl.multiple_of(s * cap, cap), cap)
            chosen = choice(s)
            gate = recv_meta[pl.ds(pl.multiple_of(8 * s, 8), 8), :][1:2, :]
            gate = jnp.sum(jnp.where(chosen, gate, 0.0), axis=1, keepdims=True)
            picked = dot(chosen.astype(F32).astype(BF16), all_cot[s], (1, 0))
            recv_cot[rows, :] = (gate * picked).astype(BF16)
    else:
        pl.loop(0, tiles)(forward)
        arrived(1, recv_cot)
    outs[...] = d_acc[...].astype(BF16)
    start_exchange(2, outs, back_out)

    half_u, half_d = width // 2, step // 2
    quart_u, quart_d = width // 4, step // 4

    def rows_of(big, index, size, small=None, inner=0):
        at = big + index * size
        if small is not None:
            at = at + inner * small
        return pl.multiple_of(at, small or size)

    def reduce_copy(phase, which, t):
        cols = pl.ds(pl.multiple_of(t * step, step), step)
        if which == 0:
            a, b = xb, yb
            first, second = (x_peer, me), (y_peer, me)
            base, half, quart = 0, half_u, quart_u
            part, one, two, final = part_up, one_up, two_up, grad_up
        else:
            a, b = yb, xb
            first, second = (y_peer, me), (x_peer, me)
            base, half, quart = t * step, half_d, quart_d
            part, one, two, final = part_down, one_down, two_down, grad_down

        def view(ref, start, size):
            rows = pl.ds(start, size)
            return ref.at[rows, cols] if which == 0 else ref.at[rows]

        if phase == 0:
            src, dst, peer = view(part, rows_of(base, 1 - a, half), half), one.at[t], first
        elif phase == 1:
            src = view(part, rows_of(base, a, half, quart, 1 - b), quart)
            dst, peer = two.at[t], second
        elif phase == 2:
            src = dst = view(final, rows_of(base, a, half, quart, b), quart)
            peer = second
        else:
            src = dst = view(final, rows_of(base, a, half), half)
            peer = first
        return pltpu.make_async_remote_copy(
            src_ref=src, dst_ref=dst,
            send_sem=ar_send.at[phase, which, t], recv_sem=ar_recv.at[phase, which, t],
            device_id=peer, device_id_type=MESH,
        )

    @pl.loop(0, tiles)
    def _(t):
        cols = pl.ds(pl.multiple_of(t * step, step), step)
        d_hidden = dot(recv_cot[...], w_down[cols, :], (1, 1))
        part_down[cols, :] = dot(hid[t], recv_cot[...], (0, 0)).astype(BF16)
        reduce_copy(0, 1, t).start()
        d_pre = (d_hidden * slope[t]).astype(BF16)
        part_up[:, cols] = dot(recv_in[...], d_pre, (0, 0)).astype(BF16)
        reduce_copy(0, 0, t).start()
        term = dot(d_pre, w_up[:, cols], (1, 1))

        @pl.when(t == 0)
        def _():
            d_acc[...] = term

        @pl.when(t > 0)
        def _():
            d_acc[...] += term

    d_ins[...] = d_acc[...].astype(BF16)
    start_exchange(3, d_ins, back_grad)

    @pl.loop(0, tiles)
    def _(t):
        cols = pl.ds(pl.multiple_of(t * step, step), step)
        reduce_copy(0, 1, t).wait_recv()
        rows = pl.ds(rows_of(t * step, yb, half_d), half_d)
        part_down[rows, :] = (part_down[rows, :].astype(F32) + one_down[t].astype(F32)).astype(BF16)
        reduce_copy(1, 1, t).start()
        reduce_copy(0, 0, t).wait_recv()
        rows = pl.ds(rows_of(0, xb, half_u), half_u)
        part_up[rows, cols] = (part_up[rows, cols].astype(F32) + one_up[t].astype(F32)).astype(BF16)
        reduce_copy(1, 0, t).start()

    @pl.loop(0, tiles)
    def _(t):
        cols = pl.ds(pl.multiple_of(t * step, step), step)
        reduce_copy(1, 1, t).wait_recv()
        rows = pl.ds(rows_of(t * step, yb, half_d, quart_d, xb), quart_d)
        grad_down[rows, :] = (part_down[rows, :].astype(F32) + two_down[t].astype(F32)).astype(BF16)
        reduce_copy(2, 1, t).start()
        reduce_copy(1, 0, t).wait_recv()
        rows = pl.ds(rows_of(0, xb, half_u, quart_u, yb), quart_u)
        grad_up[rows, cols] = (part_up[rows, cols].astype(F32) + two_up[t].astype(F32)).astype(BF16)
        reduce_copy(2, 0, t).start()

    def gathered(phase, which, t):
        cols = pl.ds(pl.multiple_of(t * step, step), step)
        a, b = (xb, yb) if which == 0 else (yb, xb)
        base, half, quart = (0, half_u, quart_u) if which == 0 else (t * step, half_d, quart_d)
        if phase == 2:
            rows = pl.ds(rows_of(base, a, half, quart, 1 - b), quart)
        else:
            rows = pl.ds(rows_of(base, 1 - a, half), half)
        ref = grad_up.at[rows, cols] if which == 0 else grad_down.at[rows]
        pltpu.make_async_remote_copy(
            src_ref=ref, dst_ref=ref,
            send_sem=ar_send.at[phase, which, t], recv_sem=ar_recv.at[phase, which, t],
            device_id=(x_peer, me), device_id_type=MESH,
        ).wait_recv()

    @pl.loop(0, tiles)
    def _(t):
        for which in (1, 0):
            gathered(2, which, t)
            reduce_copy(3, which, t).start()

    arrived(2, back_out)
    arrived(3, back_grad)
    picks = picks_of()
    gates = [gate_s[:, k : k + 1] for k in range(2)]
    squashed = [squash_s[:, k : k + 1] for k in range(2)]
    total = squashed[0] + squashed[1]
    cot_wide = cotangent[...].astype(F32)
    expert_out = [dot(pick, back_out[...], (1, 0)) for pick in picks]
    layer_out[...] = (
        mixed_s[...].astype(F32) + (gates[0] * expert_out[0] + gates[1] * expert_out[1])
    ).astype(BF16)
    d_gates = [jnp.sum(o * cot_wide, axis=1, keepdims=True) for o in expert_out]
    mean_term = gates[0] * d_gates[0] + gates[1] * d_gates[1]
    expert_ids = count((tok, n_exp), 1)
    d_logits = jnp.zeros((tok, n_exp), F32)
    for k in range(2):
        d_chosen = (d_gates[k] - mean_term) / total * squashed[k] * (1.0 - squashed[k])
        d_logits += jnp.where(route_s[:, k : k + 1] == expert_ids, d_chosen, 0.0)
    d_router = dot(d_logits, router[...].astype(F32), (1, 0), EXACT)
    slot_sum = dot(picks[0] + picks[1], back_grad[...], (1, 0))
    grad_in[...] = (cot_wide + slot_sum + d_router).astype(BF16)

    if near:
        sent(0, send_meta, recv_meta)
        passed(0)
        passed(1)
    else:
        sent(0, send_in, recv_in)
        sent(1, send_cot, recv_cot)
    sent(2, outs, back_out)
    sent(3, d_ins, back_grad)

    @pl.loop(0, tiles)
    def _(t):
        for which in (1, 0):
            gathered(3, which, t)
            for phase in range(4):
                reduce_copy(phase, which, t).wait_send()


def copy_out(*refs):
    for i in range(4):
        refs[4 + i][...] = refs[i][...]


def per_device(
    features, slots, routes, cotangent, pos_table, tower_in, tower_out, router, w_up, w_down
):
    tok, width = features.shape
    n_exp = router.shape[1]
    hidden = w_up.shape[2]
    cap = 4 * tok // n_exp
    rows = n_exp * cap
    tiles = 8
    step = hidden // tiles
    vmem = pl.BlockSpec(memory_space=pltpu.VMEM)
    dma = pltpu.SemaphoreType.DMA
    near = []
    if n_exp == 0:
        near = [
            pltpu.VMEM((n_exp, tok, width), BF16),
            pltpu.VMEM((n_exp, tok, width), BF16),
            pltpu.VMEM((n_exp * 8, tok), F32),
            pltpu.VMEM((n_exp * 8, tok), F32),
            dma((2, 3, n_exp // 2)),
            dma((2, n_exp)),
        ]
    outs = pl.pallas_call(
        functools.partial(kernel, (n_exp, cap, tiles)),
        out_shape=(
            jax.ShapeDtypeStruct((tok, width), BF16),
            jax.ShapeDtypeStruct((tok, width), BF16),
            jax.ShapeDtypeStruct((width, hidden), BF16),
            jax.ShapeDtypeStruct((hidden, width), BF16),
        ),
        in_specs=[vmem] * 10,
        out_specs=(vmem,) * 4,
        scratch_shapes=[
            pltpu.VMEM((tok, width), BF16),
            pltpu.VMEM((tok, 2), F32),
            pltpu.VMEM((tok, 2), F32),
            pltpu.VMEM((tok, 2), F32),
            pltpu.VMEM((tok, 2), F32),
            pltpu.VMEM((rows, width), BF16),
            pltpu.VMEM((rows, width), BF16),
            pltpu.VMEM((rows, width), BF16),
            pltpu.VMEM((rows, width), BF16),
            pltpu.VMEM((tiles, rows, step), BF16),
            pltpu.VMEM((tiles, rows, step), F32),
            pltpu.VMEM((rows, width), BF16),
            pltpu.VMEM((rows, width), F32),
            pltpu.VMEM((rows, width), BF16),
            pltpu.VMEM((rows, width), BF16),
            pltpu.VMEM((rows, width), BF16),
            pltpu.VMEM((width, hidden), BF16),
            pltpu.VMEM((hidden, width), BF16),
            pltpu.VMEM((tiles, width // 2, step), BF16),
            pltpu.VMEM((tiles, step // 2, width), BF16),
            pltpu.VMEM((tiles, width // 4, step), BF16),
            pltpu.VMEM((tiles, step // 4, width), BF16),
            dma((4, n_exp)),
            dma((4, n_exp)),
            dma((4, 2, tiles)),
            dma((4, 2, tiles)),
        ]
        + near,
        compiler_params=pltpu.CompilerParams(
            collective_id=0, has_side_effects=True, vmem_limit_bytes=60 * 1024 * 1024
        ),
    )(
        features, slots[None], routes.T, cotangent, pos_table, tower_in, tower_out, router.T,
        w_up[0], w_down[0],
    )
    blocks = [pl.BlockSpec((o.shape[0] // 4, o.shape[1]), lambda i: (i, 0)) for o in outs]
    outs = pl.pallas_call(
        copy_out,
        grid=(4,),
        out_shape=tuple(jax.ShapeDtypeStruct(o.shape, o.dtype) for o in outs),
        in_specs=blocks,
        out_specs=tuple(blocks),
    )(*outs)
    return outs[0], outs[1], outs[2][None], outs[3][None]


def solution(mesh):
    return jax.shard_map(
        per_device,
        mesh=mesh,
        in_specs=(
            P(("dp", "expert"), None),
            P(("dp", "expert")),
            P(("dp", "expert"), None),
            P(("dp", "expert"), None),
            P(),
            P(),
            P(),
            P(),
            P("expert", None, None),
            P("expert", None, None),
        ),
        out_specs=(
            P(("dp", "expert"), None),
            P(("dp", "expert"), None),
            P("expert", None, None),
            P("expert", None, None),
        ),
        check_vma=False,
    )
```
